32 devices in a mesh: groups: 2 (over y), ctx: 4 (over z), chan: 4 (over x, core).
Axes of the slice: x: 2, y: 2, z: 4, core: 2. Of those that a mesh axis runs over, the one named last changes fastest.
Arguments:
- query_stream: bfloat16 [4096, 2048], P('chan', ('groups', 'ctx')), parts along dimension 1, may hold values from -6 to 6
- key_stream: bfloat16 [4096, 2048], P('chan', ('groups', 'ctx')), parts along dimension 1, may hold values from -6 to 6
- value_stream: bfloat16 [4096, 2048], P('chan', ('groups', 'ctx')), parts along dimension 1, may hold values from -6 to 6
- cotangent: bfloat16 [4096, 2048], P('chan', ('groups', 'ctx')), parts along dimension 1, may hold values from -6 to 6
- filters: float32 [256, 1024], P(None, 'ctx'), may hold values from -1.5 to 1.5
Outputs:
- query_grad: bfloat16 [4096, 2048], P('chan', ('groups', 'ctx')), parts along dimension 1
- key_grad: bfloat16 [4096, 2048], P('chan', ('groups', 'ctx')), parts along dimension 1
- value_grad: bfloat16 [4096, 2048], P('chan', ('groups', 'ctx')), parts along dimension 1
- filter_grad: float32 [256, 2048], P(None, ('groups', 'ctx')), parts along dimension 1
The draws below stay inside these ranges and needn't reach their ends.
There are 2 independent parts, one for each index of `groups`. The reference program is written for one: setup_inputs(seed, part) draws one part's arguments, and reference() takes and returns one part's arrays. A program takes and returns all parts, laid end to end along the dimension named above; an argument that names none is the same for every part. Nothing has to cross between parts.
All inputs are finite; a program needn't handle non-finite values.
Results may differ from the reference program's by a relative error of at most 0.001.
Values may be sent and summed in bfloat16 or wider, within the bound.
A program may use at most 64 MiB of HBM per device.

```python
import math
import jax
import jax.numpy as jnp
from jax import lax

CH = 4096
GROUP = 16
FILT = 256
SEQ = 1024


def draw_filters(key, part):
    key = jax.random.fold_in(key, 11)
    key_order, key_rough, key_slow, key_fast = jax.random.split(key, 4)
    order = jax.random.permutation(key_order, FILT)
    positions = jnp.arange(SEQ, dtype=jnp.float32)
    slow_count = FILT // 2
    rough = jax.random.truncated_normal(key_rough, -4.0, 4.0, (FILT, SEQ), jnp.float32)
    slow_rate = jnp.exp(jax.random.uniform(key_slow, (FILT,), jnp.float32, math.log(0.2 / SEQ), math.log(2.0 / SEQ)))
    fast_rate = jnp.exp(jax.random.uniform(key_fast, (FILT,), jnp.float32, math.log(1.0 / 400.0), math.log(1.0 / 30.0)))
    rate_values = jnp.where(order < slow_count, slow_rate, fast_rate)
    amplitude = jnp.sqrt(2.0 * rate_values)
    decay_curve = jnp.exp(-rate_values[:, None] * positions[None, :])
    return (rough * amplitude[:, None] * decay_curve).astype(jnp.float32)


def level_of(rng, extent, cuts, least, largest):
    level, own = 1.0, jax.random.fold_in(rng, 6)
    for position, parts in cuts:
        heights = jnp.exp(jax.random.uniform(jax.random.fold_in(own, position), (parts,), jnp.float32, least / len(cuts), largest / len(cuts)))
        level = level * jnp.repeat(heights, extent[position] // parts).reshape([-1 if axis == position else 1 for axis in range(len(extent))])
    return level


def centred(own_key, dims, deviation, most, cuts=(), held_as=jnp.bfloat16):
    entries = deviation * jax.random.normal(own_key, dims, jnp.float32)
    if cuts:
        entries = entries * level_of(own_key, dims, cuts, -0.22, 0.18)
    return jnp.clip(entries, -most, most).astype(held_as)


def setup_inputs(seed: int = 0, part: int = 0) -> dict:
    keys = jax.random.split(jax.random.key(seed), 6)
    part_splits = jax.random.split(jax.random.fold_in(keys[5], part), 6)
    query_stream = centred(part_splits[0], (CH, SEQ), 1.0, 6.0, ((0, 4), (1, 4)))
    key_stream = centred(part_splits[1], (CH, SEQ), 1.0, 6.0, ((0, 4), (1, 4)))
    value_stream = centred(part_splits[2], (CH, SEQ), 1.0, 6.0, ((0, 4), (1, 4)))
    cotangent = centred(part_splits[3], (CH, SEQ), 1.0, 6.0, ((0, 4), (1, 4)))
    filters = draw_filters(jax.random.fold_in(keys[5], 71), part)
    return {"query_stream": query_stream, "key_stream": key_stream, "value_stream": value_stream, "cotangent": cotangent, "filters": filters}


def reference(query_stream, key_stream, value_stream, cotangent, filters):
    padded_len = 2 * SEQ
    block_count = CH // FILT
    spec_filt = jnp.fft.rfft(filters.astype(jnp.float32), n=padded_len, axis=-1)
    stacked = jnp.stack([query_stream, key_stream, value_stream, cotangent], axis=0)
    stacked = jnp.moveaxis(stacked.reshape(4, block_count, FILT, SEQ), 1, 0)

    def one_block(running, pieces):
        queries = pieces[0].astype(jnp.float32)
        key_data = pieces[1].astype(jnp.float32)
        value_data = pieces[2].astype(jnp.float32)
        cot_data = pieces[3].astype(jnp.float32)
        product = key_data * value_data
        adjoint = cot_data * queries
        spec_prod = jnp.fft.rfft(product, n=padded_len, axis=-1)
        spec_adj = jnp.fft.rfft(adjoint, n=padded_len, axis=-1)
        conv_out = jnp.fft.irfft(spec_filt * spec_prod, n=padded_len, axis=-1)[:, :SEQ]
        conv_back = jnp.fft.irfft(jnp.conj(spec_filt) * spec_adj, n=padded_len, axis=-1)[:, :SEQ]
        filter_rows = jnp.fft.irfft(spec_adj * jnp.conj(spec_prod), n=padded_len, axis=-1)[:, :SEQ]
        query_grad = (cot_data * conv_out).astype(jnp.bfloat16)
        key_grad = (conv_back * value_data).astype(jnp.bfloat16)
        value_grad = (conv_back * key_data).astype(jnp.bfloat16)
        return (running + filter_rows, jnp.stack([query_grad, key_grad, value_grad], axis=0))
    total, grads = lax.scan(one_block, jnp.zeros((FILT, SEQ), jnp.float32), stacked)
    grads = jnp.moveaxis(grads, 1, 0).reshape(3, CH, SEQ)
    filter_grad = total / math.sqrt(GROUP * SEQ)
    return (grads[0], grads[1], grads[2], filter_grad)
```

```python
import functools
import math

import jax
import jax.numpy as jnp
import numpy as np
from jax import lax
from jax.experimental import pallas as pl
from jax.experimental.pallas import tpu as pltpu
from jax.sharding import PartitionSpec as P

GROUP = 16
MESH = pl.DeviceIdType.MESH
ROWS = 16


def half_tables(block):
    span = np.arange(block, dtype=np.int64)
    turned = ((2 * span[None, :] + 1) * span[:, None]) % (4 * block)
    angle = turned.astype(np.float64) * (math.pi / (2 * block))
    ahead = np.concatenate([np.cos(angle), -np.sin(angle)], axis=1).astype(np.float32)
    back = (np.concatenate([np.cos(angle).T, -np.sin(angle).T], axis=0) / block).astype(np.float32)

    def parts(table):
        high = table.astype(jnp.bfloat16)
        low = (table - high.astype(np.float32)).astype(jnp.bfloat16)
        return high, low

    ahead_high, ahead_low = parts(ahead)
    back_high, back_low = parts(back)
    return (
        np.concatenate([ahead_high, ahead_high, ahead_low], axis=0),
        np.concatenate([back_high, back_high, back_low], axis=0),
    )


def ctx_kernel(
    nchan,
    q_ref,
    k_ref,
    v_ref,
    c_ref,
    filt_ref,
    ahead_ref,
    back_ref,
    qg_ref,
    kg_ref,
    vg_ref,
    fg_ref,
    pair_p,
    pair_a,
    landed,
    filt_all,
    gains,
    spec,
    prep,
    corr,
    agg_out,
    agg_in,
    send_sem,
    recv_sem,
    filt_send,
    filt_recv,
    spread_send,
    spread_recv,
    agg_send,
    agg_recv,
):
    local_ch, block = q_ref.shape
    fcount = filt_ref.shape[0]
    chunks = local_ch // fcount
    quarter = fcount // nchan
    me = lax.axis_index("ctx")
    mine = lax.axis_index("chan")
    f32, bf16 = jnp.float32, jnp.bfloat16

    barrier = pltpu.get_barrier_semaphore()
    for step in range(1, 4):
        pl.semaphore_signal(
            barrier, inc=1, device_id={"ctx": lax.rem(me + step, 4)}, device_id_type=MESH
        )
    for step in range(1, nchan):
        pl.semaphore_signal(
            barrier, inc=1, device_id={"chan": lax.rem(mine + step, nchan)}, device_id_type=MESH
        )

    def split_into(dest, rows, left, right):
        val = left.astype(f32) * right.astype(f32)
        high = val.astype(bf16)
        dest[rows, 0:block] = high
        dest[rows, block : 2 * block] = (val - high.astype(f32)).astype(bf16)

    @pl.loop(0, local_ch // 64)
    def _(i):
        rows = pl.ds(pl.multiple_of(i * 64, 64), 64)
        split_into(pair_p, rows, k_ref[rows, :], v_ref[rows, :])
        split_into(pair_a, rows, c_ref[rows, :], q_ref[rows, :])

    pl.semaphore_wait(barrier, 3 + nchan - 1)

    def move(source, chunk, slot, target):
        rows = pl.ds(chunk * fcount, fcount)
        return pltpu.make_async_remote_copy(
            src_ref=source.at[rows, :],
            dst_ref=landed.at[slot, rows, :],
            send_sem=send_sem.at[slot, chunk],
            recv_sem=recv_sem.at[slot, chunk],
            device_id={"ctx": target},
            device_id_type=MESH,
        )

    def filt_move(owner, target):
        rows = pl.ds(pl.multiple_of(mine * quarter, quarter), quarter)
        return pltpu.make_async_remote_copy(
            src_ref=filt_ref.at[rows, :],
            dst_ref=filt_all.at[owner, rows, :],
            send_sem=filt_send.at[target],
            recv_sem=filt_recv.at[owner],
            device_id={"ctx": target},
            device_id_type=MESH,
        )

    def spread(owner, step):
        rows = pl.ds(pl.multiple_of(mine * quarter, quarter), quarter)
        return pltpu.make_async_remote_copy(
            src_ref=filt_all.at[owner, rows, :],
            dst_ref=filt_all.at[owner, rows, :],
            send_sem=spread_send.at[owner, step],
            recv_sem=spread_recv.at[owner, step],
            device_id={"chan": lax.rem(mine + step, nchan)},
            device_id_type=MESH,
        )

    def agg_move(chunk, target):
        rows = pl.ds(chunk * fcount, fcount)
        return pltpu.make_async_remote_copy(
            src_ref=agg_out.at[rows, :],
            dst_ref=agg_in.at[rows, :],
            send_sem=agg_send.at[chunk],
            recv_sem=agg_recv.at[chunk],
            device_id={"ctx": target},
            device_id_type=MESH,
        )

    def ahead(pairs):
        high = pairs[:, 0:block]
        return jnp.dot(pairs, ahead_ref[0 : 2 * block, :], preferred_element_type=f32) + jnp.dot(
            high, ahead_ref[2 * block : 3 * block, :], preferred_element_type=f32
        )

    def inverse_of(which):
        return jnp.dot(
            prep[which, :, :], back_ref[0 : 4 * block, :], preferred_element_type=f32
        ) + jnp.dot(
            prep[which, :, 0 : 2 * block],
            back_ref[4 * block : 6 * block, :],
            preferred_element_type=f32,
        )

    def put_prep(which, rows, re, im):
        for place, val in ((0, re), (block, im)):
            high = val.astype(bf16)
            prep[which, rows, place : place + block] = high
            prep[which, rows, 2 * block + place : 3 * block + place] = (
                val - high.astype(f32)
            ).astype(bf16)

    def sign_of():
        col = lax.broadcasted_iota(jnp.int32, (ROWS, block), 1)
        return (1 - 2 * lax.rem(col, 2)).astype(f32)

    def role(j):
        inner = j in (1, 2)
        lower = j < 2
        own_u = pair_p if lower else pair_a
        sends = []
        targets = {0: (1, 2, 3), 1: (2,), 2: (1,), 3: (2, 1)}[j]
        needs = {0: (), 1: (0, 2, 3), 2: (0, 1, 3), 3: (0,)}[j]
        for target in targets:
            copy = filt_move(j, target)
            copy.start()
            sends.append(copy)
        for chunk in range(chunks):
            if inner:
                moves = [move(own_u, chunk, 1, 3 - j)]
            else:
                moves = [
                    move(own_u, chunk, 2, 2 if lower else 1),
                    move(own_u, chunk, 0, 1 if lower else 2),
                ]
            for copy in moves:
                copy.start()
                sends.append(copy)
        for owner in needs:
            filt_move(owner, j).wait_recv()
            for step in range(1, nchan):
                copy = spread(owner, step)
                copy.start()
                sends.append(copy)
        filt_all[j, :, :] = filt_ref[...]
        for owner in needs:
            for step in range(1, nchan):
                spread(owner, step).wait_recv()
        used = range(4) if inner else (0,)
        for owner in used:
            val = filt_all[owner, :, :]
            high = val.astype(bf16)
            low = (val - high.astype(f32)).astype(bf16)
            spec[owner, :, :] = ahead(jnp.concatenate([high, low], axis=1))

        @pl.loop(0, fcount // ROWS)
        def _(i):
            rows = pl.ds(pl.multiple_of(i * ROWS, ROWS), ROWS)
            sign = sign_of()
            for d in used:
                re, im = spec[d, rows, 0:block], spec[d, rows, block : 2 * block]
                if d:
                    re = re - sign * spec[d - 1, rows, block : 2 * block]
                    im = im + sign * spec[d - 1, rows, 0:block]
                gains[d, rows, 0:block] = re
                gains[d, rows, block : 2 * block] = im
                corr[d, rows, :] = jnp.zeros((ROWS, 2 * block), f32)

        if inner:
            held_p = {1: (0, 1), 2: (0, 1, 2)}[j]
            held_a = {1: (1, 2, 3), 2: (2, 3)}[j]
        else:
            held_p, held_a = (j,), (j,)
        places = {}
        for i in held_p:
            places["p", i] = len(places)
        for i in held_a:
            places["a", i] = len(places)
        slots = {1: {("p", 0): 0, ("a", 2): 1, ("a", 3): 2}, 2: {("a", 3): 0, ("p", 1): 1, ("p", 0): 2}}
        slots = slots.get(j, {})
        pairs_fg = {
            0: ((0, 0),),
            1: ((1, 1), (0, 1), (1, 2), (1, 3)),
            2: ((2, 2), (2, 3), (0, 2), (0, 3)),
            3: ((3, 3),),
        }[j]

        for chunk in range(chunks):
            crow = pl.ds(chunk * fcount, fcount)
            for name, place in places.items():
                if name in slots:
                    move(own_u, chunk, slots[name], j).wait_recv()
                    spec[place, :, :] = ahead(landed[slots[name], crow, :])
                else:
                    spec[place, :, :] = ahead((pair_p if name[0] == "p" else pair_a)[crow, :])

            @pl.loop(0, fcount // ROWS)
            def _(i):
                rows = pl.ds(pl.multiple_of(i * ROWS, ROWS), ROWS)

                def load(name):
                    at = places[name]
                    return spec[at, rows, 0:block], spec[at, rows, block : 2 * block]

                def gain(d):
                    return gains[d, rows, 0:block], gains[d, rows, block : 2 * block]

                def mixed_to(target):
                    re = im = None
                    for src in held_p:
                        if src > target:
                            continue
                        pr, pi = load(("p", src))
                        gr, gi = gain(target - src)
                        r, m = pr * gr - pi * gi, pr * gi + pi * gr
                        re, im = (r, m) if re is None else (re + r, im + m)
                    return re, im

                def back_to(target):
                    re = im = None
                    for src in held_a:
                        if src < target:
                            continue
                        ar, ai = load(("a", src))
                        gr, gi = gain(src - target)
                        r, m = ar * gr + ai * gi, ai * gr - ar * gi
                        re, im = (r, m) if re is None else (re + r, im + m)
                    return re, im

                put_prep(0, rows, *mixed_to(j))
                put_prep(1, rows, *back_to(j))
                if j == 1:
                    put_prep(2, rows, *back_to(0))
                if j == 2:
                    put_prep(2, rows, *mixed_to(3))
                for src, dst in pairs_fg:
                    pr, pi = load(("p", src))
                    ar, ai = load(("a", dst))
                    d = dst - src
                    corr[d, rows, 0:block] += ar * pr + ai * pi
                    corr[d, rows, block : 2 * block] += ai * pr - ar * pi

            if inner:
                agg_out[crow, :] = inverse_of(2)
                copy = agg_move(chunk, 0 if lower else 3)
                copy.start()
                sends.append(copy)
            if j == 3:
                agg_out[crow, :] = inverse_of(0)
            else:
                qg_ref[crow, :] = (c_ref[crow, :].astype(f32) * inverse_of(0)).astype(bf16)
            if j == 0:
                agg_out[crow, :] = inverse_of(1)
            else:
                back = inverse_of(1)
                kg_ref[crow, :] = (back * v_ref[crow, :].astype(f32)).astype(bf16)
                vg_ref[crow, :] = (back * k_ref[crow, :].astype(f32)).astype(bf16)

        scale = 1.0 / math.sqrt(GROUP * block * 4)
        for b in range(4):
            if b not in used:
                fg_ref[b, :, :] = jnp.zeros((fcount, block), f32)
                continue

            @pl.loop(0, fcount // ROWS)
            def _(i):
                rows = pl.ds(pl.multiple_of(i * ROWS, ROWS), ROWS)
                re, im = corr[b, rows, 0:block], corr[b, rows, block : 2 * block]
                if b + 1 in used:
                    sign = sign_of()
                    re = re + sign * corr[b + 1, rows, block : 2 * block]
                    im = im - sign * corr[b + 1, rows, 0:block]
                put_prep(0, rows, re, im)

            fg_ref[b, :, :] = inverse_of(0) * scale

        if not inner:
            for chunk in range(chunks):
                crow = pl.ds(chunk * fcount, fcount)
                agg_move(chunk, j).wait_recv()
                total = agg_out[crow, :] + agg_in[crow, :]
                if j == 3:
                    qg_ref[crow, :] = (c_ref[crow, :].astype(f32) * total).astype(bf16)
                else:
                    kg_ref[crow, :] = (total * v_ref[crow, :].astype(f32)).astype(bf16)
                    vg_ref[crow, :] = (total * k_ref[crow, :].astype(f32)).astype(bf16)
        for copy in sends:
            copy.wait_send()

    for j in range(4):
        pl.when(me == j)(functools.partial(role, j))


def blocked_body(query_stream, key_stream, value_stream, cotangent, filters):
    local_ch, block = query_stream.shape
    fcount = filters.shape[0]
    nchan = lax.axis_size("chan")
    chunks = local_ch // fcount
    ahead, back = half_tables(block)
    ahead = jnp.asarray(ahead)
    back = jnp.asarray(back)
    vmem = pl.BlockSpec(memory_space=pltpu.VMEM)
    stream = jax.ShapeDtypeStruct((local_ch, block), jnp.bfloat16)
    dma = pltpu.SemaphoreType.DMA
    query_grad, key_grad, value_grad, terms = pl.pallas_call(
        functools.partial(ctx_kernel, nchan),
        out_shape=(
            stream,
            stream,
            stream,
            jax.ShapeDtypeStruct((4, fcount, block), jnp.float32),
        ),
        in_specs=[vmem] * 7,
        out_specs=(vmem,) * 4,
        scratch_shapes=[
            pltpu.VMEM((local_ch, 2 * block), jnp.bfloat16),
            pltpu.VMEM((local_ch, 2 * block), jnp.bfloat16),
            pltpu.VMEM((3, local_ch, 2 * block), jnp.bfloat16),
            pltpu.VMEM((4, fcount, block), jnp.float32),
            pltpu.VMEM((4, fcount, 2 * block), jnp.float32),
            pltpu.VMEM((5, fcount, 2 * block), jnp.float32),
            pltpu.VMEM((3, fcount, 4 * block), jnp.bfloat16),
            pltpu.VMEM((4, fcount, 2 * block), jnp.float32),
            pltpu.VMEM((local_ch, block), jnp.float32),
            pltpu.VMEM((local_ch, block), jnp.float32),
            dma((3, chunks)),
            dma((3, chunks)),
            dma((4,)),
            dma((4,)),
            dma((4, nchan)),
            dma((4, nchan)),
            dma((chunks,)),
            dma((chunks,)),
        ],
        compiler_params=pltpu.CompilerParams(
            collective_id=0, has_side_effects=True, vmem_limit_bytes=48 * 1024 * 1024
        ),
        cost_estimate=pl.CostEstimate(flops=8 * 10**9, bytes_accessed=8 * 10**6, transcendentals=0),
    )(query_stream, key_stream, value_stream, cotangent, filters, ahead, back)
    summed = lax.psum_scatter(terms, "ctx", scatter_dimension=0, tiled=True)
    filter_grad = lax.psum(summed.reshape(fcount, block), "chan")
    return (query_grad, key_grad, value_grad, filter_grad)


highest_mode = lax.Precision.HIGHEST


def turn_table(row_count, col_count, modulus):
    row_span = jnp.arange(row_count, dtype=jnp.int32)
    col_span = jnp.arange(col_count, dtype=jnp.int32)
    turned = row_span[:, None] * col_span[None, :] % modulus
    angle_vals = turned.astype(jnp.float32) * (2.0 * math.pi / modulus)
    return (jnp.cos(angle_vals), jnp.sin(angle_vals))


def split_of(length):
    for candidate in range(32, 1, -1):
        if (
            length % candidate == 0
            and length // candidate >= 128
            and (length // candidate % 128 == 0)
        ):
            return candidate
    return 1


def contract_front(table, operand):
    return jnp.einsum("ac,...ab->...cb", table, operand, precision=highest_mode)


def base_transform(re_part, im_part, sign_value):
    length = re_part.shape[-1]
    cos_table, sin_table = turn_table(length, length, length)
    turn_imag = sign_value * sin_table
    summed = jnp.einsum("...t,tk->...k", re_part + im_part, cos_table, precision=highest_mode)
    left_term = jnp.einsum("...t,tk->...k", re_part, turn_imag - cos_table, precision=highest_mode)
    second = jnp.einsum("...t,tk->...k", im_part, cos_table + turn_imag, precision=highest_mode)
    return (summed - second, summed + left_term)


def twist_forward(y_real, y_imag, length, leading):
    radix_size, inner_len = y_real.shape[-2:]
    cos_twist, sin_twist = turn_table(radix_size, inner_len, length)
    tw_real = y_real * cos_twist + y_imag * sin_twist
    tw_imag = y_imag * cos_twist - y_real * sin_twist
    z_real, z_imag = forward(tw_real, tw_imag)
    return (z_real.reshape(leading + (length,)), z_imag.reshape(leading + (length,)))


def forward(re_part, im_part):
    length = re_part.shape[-1]
    leading = re_part.shape[:-1]
    radix_size = split_of(length)
    if radix_size == 1:
        return base_transform(re_part, im_part, -1.0)
    inner_len = length // radix_size
    re_grid = re_part.reshape(leading + (radix_size, inner_len))
    im_grid = im_part.reshape(leading + (radix_size, inner_len))
    cos_table, sin_table = turn_table(radix_size, radix_size, radix_size)
    y_real = contract_front(cos_table, re_grid) + contract_front(sin_table, im_grid)
    y_imag = contract_front(cos_table, im_grid) - contract_front(sin_table, re_grid)
    return twist_forward(y_real, y_imag, length, leading)


def forward_padded(signal):
    half_len = signal.shape[-1]
    length = 2 * half_len
    leading = signal.shape[:-1]
    radix_size = split_of(length)
    inner_len = length // radix_size
    grid = signal.reshape(leading + (radix_size // 2, inner_len))
    cos_table, sin_table = turn_table(radix_size // 2, radix_size, radix_size)
    y_real = contract_front(cos_table, grid)
    y_imag = -contract_front(sin_table, grid)
    return twist_forward(y_real, y_imag, length, leading)


def untwist(z_real, z_imag, length):
    radix_size, inner_len = z_real.shape[-2:]
    cos_twist, sin_twist = turn_table(radix_size, inner_len, length)
    return (z_real * cos_twist - z_imag * sin_twist, z_imag * cos_twist + z_real * sin_twist)


def inverse(re_part, im_part):
    length = re_part.shape[-1]
    leading = re_part.shape[:-1]
    radix_size = split_of(length)
    if radix_size == 1:
        return base_transform(re_part, im_part, 1.0)
    inner_len = length // radix_size
    z_real, z_imag = inverse(
        re_part.reshape(leading + (radix_size, inner_len)),
        im_part.reshape(leading + (radix_size, inner_len)),
    )
    y_real, y_imag = untwist(z_real, z_imag, length)
    cos_table, sin_table = turn_table(radix_size, radix_size, radix_size)
    x_real = contract_front(cos_table, y_real) - contract_front(sin_table, y_imag)
    x_imag = contract_front(cos_table, y_imag) + contract_front(sin_table, y_real)
    return (x_real.reshape(leading + (length,)), x_imag.reshape(leading + (length,)))


def inverse_half(re_part, im_part):
    length = re_part.shape[-1]
    leading = re_part.shape[:-1]
    radix_size = split_of(length)
    inner_len = length // radix_size
    z_real, z_imag = inverse(
        re_part.reshape(leading + (radix_size, inner_len)),
        im_part.reshape(leading + (radix_size, inner_len)),
    )
    y_real, y_imag = untwist(z_real, z_imag, length)
    cos_table, sin_table = turn_table(radix_size, radix_size // 2, radix_size)
    x_real = contract_front(cos_table, y_real) - contract_front(sin_table, y_imag)
    x_imag = contract_front(cos_table, y_imag) + contract_front(sin_table, y_real)
    return (x_real.reshape(leading + (length // 2,)), x_imag.reshape(leading + (length // 2,)))


def body(query_stream, key_stream, value_stream, cotangent, filters):
    local_ch, length = query_stream.shape
    filter_count = filters.shape[0]
    ctx_count = lax.axis_size("ctx")
    per_device = local_ch // ctx_count
    seq_len = length * ctx_count
    padded_len = 2 * seq_len
    streams = jnp.stack([query_stream, key_stream, value_stream, cotangent], axis=0)
    arrived = lax.all_to_all(streams, "ctx", split_axis=1, concat_axis=2, tiled=True)
    queries = arrived[0].astype(jnp.float32)
    key_data = arrived[1].astype(jnp.float32)
    value_data = arrived[2].astype(jnp.float32)
    cot_data = arrived[3].astype(jnp.float32)
    repeated = jnp.tile(filters, (local_ch // filter_count, 1))
    filter_full = lax.all_to_all(repeated, "ctx", split_axis=0, concat_axis=1, tiled=True)
    product = key_data * value_data
    adjoint = cot_data * queries
    spec_real, spec_imag = forward_padded(jnp.concatenate([product, adjoint, filter_full], axis=0))
    prod_real, prod_imag = (spec_real[:per_device], spec_imag[:per_device])
    adj_real = spec_real[per_device : 2 * per_device]
    adj_imag = spec_imag[per_device : 2 * per_device]
    filt_real, filt_imag = (spec_real[2 * per_device :], spec_imag[2 * per_device :])
    mix_real = filt_real * prod_real - filt_imag * prod_imag
    mix_imag = filt_real * prod_imag + filt_imag * prod_real
    back_real = filt_real * adj_real + filt_imag * adj_imag
    back_imag = filt_real * adj_imag - filt_imag * adj_real
    corr_real = adj_real * prod_real + adj_imag * prod_imag
    corr_imag = adj_imag * prod_real - adj_real * prod_imag
    joint_real = jnp.concatenate([mix_real - back_imag, corr_real], axis=0)
    joint_imag = jnp.concatenate([mix_imag + back_real, corr_imag], axis=0)
    out_real, out_imag = inverse_half(joint_real, joint_imag)
    inv_scale = 1.0 / padded_len
    conv_out = out_real[:per_device] * inv_scale
    conv_back = out_imag[:per_device] * inv_scale
    filter_rows = out_real[per_device:] * inv_scale
    returned = lax.all_to_all(
        jnp.stack([conv_out, conv_back], axis=0), "ctx", split_axis=2, concat_axis=1, tiled=True
    )
    query_grad = (cotangent.astype(jnp.float32) * returned[0]).astype(jnp.bfloat16)
    key_grad = (returned[1] * value_stream.astype(jnp.float32)).astype(jnp.bfloat16)
    value_grad = (returned[1] * key_stream.astype(jnp.float32)).astype(jnp.bfloat16)
    grad_scale = 1.0 / math.sqrt(GROUP * seq_len)
    base_rows = lax.all_to_all(filter_rows, "ctx", split_axis=1, concat_axis=0, tiled=True)
    folded = base_rows.reshape(local_ch // filter_count, filter_count, length).sum(axis=0)
    filter_grad = lax.psum(folded, "chan") * grad_scale
    return (query_grad, key_grad, value_grad, filter_grad)


def solution(mesh):
    in_specs = (
        P("chan", ("groups", "ctx")),
        P("chan", ("groups", "ctx")),
        P("chan", ("groups", "ctx")),
        P("chan", ("groups", "ctx")),
        P(None, "ctx"),
    )
    out_specs = (
        P("chan", ("groups", "ctx")),
        P("chan", ("groups", "ctx")),
        P("chan", ("groups", "ctx")),
        P(None, ("groups", "ctx")),
    )
    chosen = body
    if mesh.shape["ctx"] == 4:
        chosen = blocked_body
    return jax.shard_map(chosen, mesh=mesh, in_specs=in_specs, out_specs=out_specs, check_vma=False)
```

```python
import functools
import math

import jax
import jax.numpy as jnp
import numpy as np
from jax import lax
from jax.experimental import pallas as pl
from jax.experimental.pallas import tpu as pltpu
from jax.sharding import PartitionSpec as P

GROUP = 16
MESH = pl.DeviceIdType.MESH
ROWS = 16


def half_tables(block):
    span = np.arange(block, dtype=np.int64)
    turned = ((2 * span[None, :] + 1) * span[:, None]) % (4 * block)
    angle = turned.astype(np.float64) * (math.pi / (2 * block))
    ahead = np.concatenate([np.cos(angle), -np.sin(angle)], axis=1).astype(np.float32)
    back = (np.concatenate([np.cos(angle).T, -np.sin(angle).T], axis=0) / block).astype(np.float32)

    def parts(table):
        high = table.astype(jnp.bfloat16)
        low = (table - high.astype(np.float32)).astype(jnp.bfloat16)
        return high, low

    ahead_high, ahead_low = parts(ahead)
    back_high, back_low = parts(back)
    return (
        np.concatenate([ahead_high, ahead_high, ahead_low], axis=0),
        np.concatenate([back_high, back_high, back_low], axis=0),
    )


def ctx_kernel(
    nchan,
    q_far,
    k_far,
    v_far,
    c_far,
    filt_far,
    ahead_far,
    back_far,
    qg_ref,
    kg_ref,
    vg_ref,
    fg_ref,
    q_ref,
    k_ref,
    v_ref,
    c_ref,
    filt_ref,
    ahead_ref,
    back_ref,
    fg_loc,
    fg_stage,
    fg_part,
    fg_ctx,
    fg_fin,
    pair_p,
    pair_a,
    landed,
    filt_all,
    gains,
    spec,
    prep,
    corr,
    agg_out,
    agg_in,
    send_sem,
    recv_sem,
    filt_send,
    filt_recv,
    spread_send,
    spread_recv,
    agg_send,
    agg_recv,
    near_sem,
    sum_send,
    sum_recv,
    own_send,
    own_recv,
    fin_send,
    fin_recv,
):
    local_ch, block = q_ref.shape
    fcount = filt_ref.shape[0]
    chunks = local_ch // fcount
    quarter = fcount // nchan
    me = lax.axis_index("ctx")
    mine = lax.axis_index("chan")
    f32, bf16 = jnp.float32, jnp.bfloat16

    near = [
        pltpu.make_async_copy(src, dst, near_sem.at[at])
        for at, (src, dst) in enumerate(
            (
                (filt_far, filt_ref),
                (k_far, k_ref),
                (v_far, v_ref),
                (c_far, c_ref),
                (q_far, q_ref),
                (ahead_far, ahead_ref),
                (back_far, back_ref),
            )
        )
    ]
    for copy in near:
        copy.start()
    barrier = pltpu.get_barrier_semaphore()
    for step in range(1, 4):
        pl.semaphore_signal(
            barrier, inc=1, device_id={"ctx": lax.rem(me + step, 4)}, device_id_type=MESH
        )
    for step in range(1, nchan):
        pl.semaphore_signal(
            barrier, inc=1, device_id={"chan": lax.rem(mine + step, nchan)}, device_id_type=MESH
        )

    def split_into(dest, rows, left, right):
        val = left.astype(f32) * right.astype(f32)
        high = val.astype(bf16)
        dest[rows, 0:block] = high
        dest[rows, block : 2 * block] = (val - high.astype(f32)).astype(bf16)

    def make_pairs(dest, left, right, chunk):
        @pl.loop(0, fcount // 64)
        def _(i):
            rows = pl.ds(pl.multiple_of(chunk * fcount + i * 64, 64), 64)
            split_into(dest, rows, left[rows, :], right[rows, :])

    for copy in near[:5]:
        copy.wait()
    pl.semaphore_wait(barrier, 3 + nchan - 1)

    def move(source, chunk, slot, target):
        rows = pl.ds(chunk * fcount, fcount)
        return pltpu.make_async_remote_copy(
            src_ref=source.at[rows, :],
            dst_ref=landed.at[slot, rows, :],
            send_sem=send_sem.at[slot, chunk],
            recv_sem=recv_sem.at[slot, chunk],
            device_id={"ctx": target},
            device_id_type=MESH,
        )

    def filt_move(owner, target):
        rows = pl.ds(pl.multiple_of(mine * quarter, quarter), quarter)
        return pltpu.make_async_remote_copy(
            src_ref=filt_ref.at[rows, :],
            dst_ref=filt_all.at[owner, rows, :],
            send_sem=filt_send.at[target],
            recv_sem=filt_recv.at[owner],
            device_id={"ctx": target},
            device_id_type=MESH,
        )

    def spread(owner, step):
        rows = pl.ds(pl.multiple_of(mine * quarter, quarter), quarter)
        return pltpu.make_async_remote_copy(
            src_ref=filt_all.at[owner, rows, :],
            dst_ref=filt_all.at[owner, rows, :],
            send_sem=spread_send.at[owner, step],
            recv_sem=spread_recv.at[owner, step],
            device_id={"chan": lax.rem(mine + step, nchan)},
            device_id_type=MESH,
        )

    def agg_move(chunk, target):
        rows = pl.ds(chunk * fcount, fcount)
        return pltpu.make_async_remote_copy(
            src_ref=agg_out.at[rows, :],
            dst_ref=agg_in.at[rows, :],
            send_sem=agg_send.at[chunk],
            recv_sem=agg_recv.at[chunk],
            device_id={"ctx": target},
            device_id_type=MESH,
        )

    def sum_move(blocks, step):
        peer = lax.rem(mine + step, nchan)
        rows = pl.ds(pl.multiple_of(peer * quarter, quarter), quarter)
        return pltpu.make_async_remote_copy(
            src_ref=fg_loc.at[blocks, rows, :],
            dst_ref=fg_stage.at[step, blocks, :, :],
            send_sem=sum_send.at[step],
            recv_sem=sum_recv.at[step],
            device_id={"chan": peer},
            device_id_type=MESH,
        )

    def own_move(target, source):
        return pltpu.make_async_remote_copy(
            src_ref=fg_part.at[target],
            dst_ref=fg_ctx.at[source],
            send_sem=own_send.at[target],
            recv_sem=own_recv.at[source],
            device_id={"ctx": target},
            device_id_type=MESH,
        )

    def fin_move(step):
        rows = pl.ds(pl.multiple_of(mine * quarter, quarter), quarter)
        return pltpu.make_async_remote_copy(
            src_ref=fg_fin.at[rows, :],
            dst_ref=fg_fin.at[rows, :],
            send_sem=fin_send.at[step],
            recv_sem=fin_recv.at[step],
            device_id={"chan": lax.rem(mine + step, nchan)},
            device_id_type=MESH,
        )

    def ahead(pairs):
        high = pairs[:, 0:block]
        return jnp.dot(pairs, ahead_ref[0 : 2 * block, :], preferred_element_type=f32) + jnp.dot(
            high, ahead_ref[2 * block : 3 * block, :], preferred_element_type=f32
        )

    def inverse_of(which):
        return jnp.dot(
            prep[which, :, :], back_ref[0 : 4 * block, :], preferred_element_type=f32
        ) + jnp.dot(
            prep[which, :, 0 : 2 * block],
            back_ref[4 * block : 6 * block, :],
            preferred_element_type=f32,
        )

    def put_prep(which, rows, re, im):
        for place, val in ((0, re), (block, im)):
            high = val.astype(bf16)
            prep[which, rows, place : place + block] = high
            prep[which, rows, 2 * block + place : 3 * block + place] = (
                val - high.astype(f32)
            ).astype(bf16)

    def sign_of():
        col = lax.broadcasted_iota(jnp.int32, (ROWS, block), 1)
        return (1 - 2 * lax.rem(col, 2)).astype(f32)

    def role(j):
        inner = j in (1, 2)
        lower = j < 2
        own_u = pair_p if lower else pair_a
        sends = []
        targets = {0: (1, 2, 3), 1: (2,), 2: (1,), 3: (2, 1)}[j]
        needs = {0: (), 1: (0, 2, 3), 2: (0, 1, 3), 3: (0,)}[j]
        for target in targets:
            copy = filt_move(j, target)
            copy.start()
            sends.append(copy)
        from_p, from_a = (pair_p, k_ref, v_ref), (pair_a, c_ref, q_ref)
        first, second = (from_p, from_a) if lower else (from_a, from_p)
        for chunk in range(chunks):
            make_pairs(*first, chunk)
            if inner:
                moves = [move(own_u, chunk, 1, 3 - j)]
            else:
                moves = [
                    move(own_u, chunk, 2, 2 if lower else 1),
                    move(own_u, chunk, 0, 1 if lower else 2),
                ]
            for copy in moves:
                copy.start()
                sends.append(copy)
        for chunk in range(chunks):
            make_pairs(*second, chunk)
        for copy in near[5:]:
            copy.wait()
        for owner in needs:
            filt_move(owner, j).wait_recv()
            for step in range(1, nchan):
                copy = spread(owner, step)
                copy.start()
                sends.append(copy)
        filt_all[j, :, :] = filt_ref[...]
        for owner in needs:
            for step in range(1, nchan):
                spread(owner, step).wait_recv()
        used = range(4) if inner else (0,)
        for owner in used:
            val = filt_all[owner, :, :]
            high = val.astype(bf16)
            low = (val - high.astype(f32)).astype(bf16)
            spec[owner, :, :] = ahead(jnp.concatenate([high, low], axis=1))

        @pl.loop(0, fcount // ROWS)
        def _(i):
            rows = pl.ds(pl.multiple_of(i * ROWS, ROWS), ROWS)
            sign = sign_of()
            for d in used:
                re, im = spec[d, rows, 0:block], spec[d, rows, block : 2 * block]
                if d:
                    re = re - sign * spec[d - 1, rows, block : 2 * block]
                    im = im + sign * spec[d - 1, rows, 0:block]
                gains[d, rows, 0:block] = re
                gains[d, rows, block : 2 * block] = im
                corr[d, rows, :] = jnp.zeros((ROWS, 2 * block), f32)

        if inner:
            held_p = {1: (0, 1), 2: (0, 1, 2)}[j]
            held_a = {1: (1, 2, 3), 2: (2, 3)}[j]
        else:
            held_p, held_a = (j,), (j,)
        places = {}
        for i in held_p:
            places["p", i] = len(places)
        for i in held_a:
            places["a", i] = len(places)
        slots = {1: {("p", 0): 0, ("a", 2): 1, ("a", 3): 2}, 2: {("a", 3): 0, ("p", 1): 1, ("p", 0): 2}}
        slots = slots.get(j, {})
        pairs_fg = {
            0: ((0, 0),),
            1: ((1, 1), (0, 1), (1, 2), (1, 3)),
            2: ((2, 2), (2, 3), (0, 2), (0, 3)),
            3: ((3, 3),),
        }[j]

        for chunk in range(chunks):
            crow = pl.ds(chunk * fcount, fcount)
            for name, place in places.items():
                if name in slots:
                    move(own_u, chunk, slots[name], j).wait_recv()
                    spec[place, :, :] = ahead(landed[slots[name], crow, :])
                else:
                    spec[place, :, :] = ahead((pair_p if name[0] == "p" else pair_a)[crow, :])

            @pl.loop(0, fcount // ROWS)
            def _(i):
                rows = pl.ds(pl.multiple_of(i * ROWS, ROWS), ROWS)

                def load(name):
                    at = places[name]
                    return spec[at, rows, 0:block], spec[at, rows, block : 2 * block]

                def gain(d):
                    return gains[d, rows, 0:block], gains[d, rows, block : 2 * block]

                def mixed_to(target):
                    re = im = None
                    for src in held_p:
                        if src > target:
                            continue
                        pr, pi = load(("p", src))
                        gr, gi = gain(target - src)
                        r, m = pr * gr - pi * gi, pr * gi + pi * gr
                        re, im = (r, m) if re is None else (re + r, im + m)
                    return re, im

                def back_to(target):
                    re = im = None
                    for src in held_a:
                        if src < target:
                            continue
                        ar, ai = load(("a", src))
                        gr, gi = gain(src - target)
                        r, m = ar * gr + ai * gi, ai * gr - ar * gi
                        re, im = (r, m) if re is None else (re + r, im + m)
                    return re, im

                put_prep(0, rows, *mixed_to(j))
                put_prep(1, rows, *back_to(j))
                if j == 1:
                    put_prep(2, rows, *back_to(0))
                if j == 2:
                    put_prep(2, rows, *mixed_to(3))
                for src, dst in pairs_fg:
                    pr, pi = load(("p", src))
                    ar, ai = load(("a", dst))
                    d = dst - src
                    corr[d, rows, 0:block] += ar * pr + ai * pi
                    corr[d, rows, block : 2 * block] += ai * pr - ar * pi

            if inner:
                agg_out[crow, :] = inverse_of(2)
                copy = agg_move(chunk, 0 if lower else 3)
                copy.start()
                sends.append(copy)
            if j == 3:
                agg_out[crow, :] = inverse_of(0)
            else:
                qg_ref[crow, :] = (c_ref[crow, :].astype(f32) * inverse_of(0)).astype(bf16)
            if j == 0:
                agg_out[crow, :] = inverse_of(1)
            else:
                back = inverse_of(1)
                kg_ref[crow, :] = (back * v_ref[crow, :].astype(f32)).astype(bf16)
                vg_ref[crow, :] = (back * k_ref[crow, :].astype(f32)).astype(bf16)

        scale = 1.0 / math.sqrt(GROUP * block * 4)
        for b in used:

            @pl.loop(0, fcount // ROWS)
            def _(i):
                rows = pl.ds(pl.multiple_of(i * ROWS, ROWS), ROWS)
                re, im = corr[b, rows, 0:block], corr[b, rows, block : 2 * block]
                if b + 1 in used:
                    sign = sign_of()
                    re = re + sign * corr[b + 1, rows, block : 2 * block]
                    im = im - sign * corr[b + 1, rows, 0:block]
                put_prep(0, rows, re, im)

            fg_loc[b, :, :] = inverse_of(0) * scale
        blocks = pl.ds(0, len(used))
        for step in range(1, nchan):
            copy = sum_move(blocks, step)
            copy.start()
            sends.append(copy)
        my_rows = pl.ds(pl.multiple_of(mine * quarter, quarter), quarter)
        for step in range(1, nchan):
            sum_move(blocks, step).wait_recv()
        for b in used:
            total = fg_loc[b, my_rows, :]
            for step in range(1, nchan):
                total = total + fg_stage[step, b, :, :]
            fg_part[b, :, :] = total
        for b in used:
            if b != j:
                copy = own_move(b, j)
                copy.start()
                sends.append(copy)

        if not inner:
            for chunk in range(chunks):
                crow = pl.ds(chunk * fcount, fcount)
                agg_move(chunk, j).wait_recv()
                total = agg_out[crow, :] + agg_in[crow, :]
                if j == 3:
                    qg_ref[crow, :] = (c_ref[crow, :].astype(f32) * total).astype(bf16)
                else:
                    kg_ref[crow, :] = (total * v_ref[crow, :].astype(f32)).astype(bf16)
                    vg_ref[crow, :] = (total * k_ref[crow, :].astype(f32)).astype(bf16)
        total = fg_part[j, :, :] if j in used else None
        for src in {0: (1, 2, 3), 1: (2,), 2: (1,), 3: (1, 2)}[j]:
            own_move(j, src).wait_recv()
            term = fg_ctx[src, :, :]
            total = term if total is None else total + term
        fg_fin[my_rows, :] = total
        for step in range(1, nchan):
            copy = fin_move(step)
            copy.start()
            sends.append(copy)
        for step in range(1, nchan):
            fin_move(step).wait_recv()
        fg_ref[...] = fg_fin[...]
        for copy in sends:
            copy.wait_send()

    for j in range(4):
        pl.when(me == j)(functools.partial(role, j))


def blocked_body(query_stream, key_stream, value_stream, cotangent, filters):
    local_ch, block = query_stream.shape
    fcount = filters.shape[0]
    nchan = lax.axis_size("chan")
    chunks = local_ch // fcount
    ahead, back = half_tables(block)
    ahead = jnp.asarray(ahead)
    back = jnp.asarray(back)
    vmem = pl.BlockSpec(memory_space=pltpu.VMEM)
    stream = jax.ShapeDtypeStruct((local_ch, block), jnp.bfloat16)
    dma = pltpu.SemaphoreType.DMA
    quarter = fcount // nchan
    return pl.pallas_call(
        functools.partial(ctx_kernel, nchan),
        out_shape=(
            stream,
            stream,
            stream,
            jax.ShapeDtypeStruct((fcount, block), jnp.float32),
        ),
        in_specs=[pl.BlockSpec(memory_space=pltpu.HBM)] * 7,
        out_specs=(vmem,) * 4,
        scratch_shapes=[
            pltpu.VMEM((local_ch, block), jnp.bfloat16),
            pltpu.VMEM((local_ch, block), jnp.bfloat16),
            pltpu.VMEM((local_ch, block), jnp.bfloat16),
            pltpu.VMEM((local_ch, block), jnp.bfloat16),
            pltpu.VMEM((fcount, block), jnp.float32),
            pltpu.VMEM((3 * block, 2 * block), jnp.bfloat16),
            pltpu.VMEM((6 * block, block), jnp.bfloat16),
            pltpu.VMEM((4, fcount, block), jnp.float32),
            pltpu.VMEM((nchan, 4, quarter, block), jnp.float32),
            pltpu.VMEM((4, quarter, block), jnp.float32),
            pltpu.VMEM((4, quarter, block), jnp.float32),
            pltpu.VMEM((fcount, block), jnp.float32),
            pltpu.VMEM((local_ch, 2 * block), jnp.bfloat16),
            pltpu.VMEM((local_ch, 2 * block), jnp.bfloat16),
            pltpu.VMEM((3, local_ch, 2 * block), jnp.bfloat16),
            pltpu.VMEM((4, fcount, block), jnp.float32),
            pltpu.VMEM((4, fcount, 2 * block), jnp.float32),
            pltpu.VMEM((5, fcount, 2 * block), jnp.float32),
            pltpu.VMEM((3, fcount, 4 * block), jnp.bfloat16),
            pltpu.VMEM((4, fcount, 2 * block), jnp.float32),
            pltpu.VMEM((local_ch, block), jnp.float32),
            pltpu.VMEM((local_ch, block), jnp.float32),
            dma((3, chunks)),
            dma((3, chunks)),
            dma((4,)),
            dma((4,)),
            dma((4, nchan)),
            dma((4, nchan)),
            dma((chunks,)),
            dma((chunks,)),
            dma((7,)),
            dma((nchan,)),
            dma((nchan,)),
            dma((4,)),
            dma((4,)),
            dma((nchan,)),
            dma((nchan,)),
        ],
        compiler_params=pltpu.CompilerParams(
            collective_id=0, has_side_effects=True, vmem_limit_bytes=60 * 1024 * 1024
        ),
        cost_estimate=pl.CostEstimate(flops=8 * 10**9, bytes_accessed=8 * 10**6, transcendentals=0),
    )(query_stream, key_stream, value_stream, cotangent, filters, ahead, back)


highest_mode = lax.Precision.HIGHEST


def turn_table(row_count, col_count, modulus):
    row_span = jnp.arange(row_count, dtype=jnp.int32)
    col_span = jnp.arange(col_count, dtype=jnp.int32)
    turned = row_span[:, None] * col_span[None, :] % modulus
    angle_vals = turned.astype(jnp.float32) * (2.0 * math.pi / modulus)
    return (jnp.cos(angle_vals), jnp.sin(angle_vals))


def split_of(length):
    for candidate in range(32, 1, -1):
        if (
            length % candidate == 0
            and length // candidate >= 128
            and (length // candidate % 128 == 0)
        ):
            return candidate
    return 1


def contract_front(table, operand):
    return jnp.einsum("ac,...ab->...cb", table, operand, precision=highest_mode)


def base_transform(re_part, im_part, sign_value):
    length = re_part.shape[-1]
    cos_table, sin_table = turn_table(length, length, length)
    turn_imag = sign_value * sin_table
    summed = jnp.einsum("...t,tk->...k", re_part + im_part, cos_table, precision=highest_mode)
    left_term = jnp.einsum("...t,tk->...k", re_part, turn_imag - cos_table, precision=highest_mode)
    second = jnp.einsum("...t,tk->...k", im_part, cos_table + turn_imag, precision=highest_mode)
    return (summed - second, summed + left_term)


def twist_forward(y_real, y_imag, length, leading):
    radix_size, inner_len = y_real.shape[-2:]
    cos_twist, sin_twist = turn_table(radix_size, inner_len, length)
    tw_real = y_real * cos_twist + y_imag * sin_twist
    tw_imag = y_imag * cos_twist - y_real * sin_twist
    z_real, z_imag = forward(tw_real, tw_imag)
    return (z_real.reshape(leading + (length,)), z_imag.reshape(leading + (length,)))


def forward(re_part, im_part):
    length = re_part.shape[-1]
    leading = re_part.shape[:-1]
    radix_size = split_of(length)
    if radix_size == 1:
        return base_transform(re_part, im_part, -1.0)
    inner_len = length // radix_size
    re_grid = re_part.reshape(leading + (radix_size, inner_len))
    im_grid = im_part.reshape(leading + (radix_size, inner_len))
    cos_table, sin_table = turn_table(radix_size, radix_size, radix_size)
    y_real = contract_front(cos_table, re_grid) + contract_front(sin_table, im_grid)
    y_imag = contract_front(cos_table, im_grid) - contract_front(sin_table, re_grid)
    return twist_forward(y_real, y_imag, length, leading)


def forward_padded(signal):
    half_len = signal.shape[-1]
    length = 2 * half_len
    leading = signal.shape[:-1]
    radix_size = split_of(length)
    inner_len = length // radix_size
    grid = signal.reshape(leading + (radix_size // 2, inner_len))
    cos_table, sin_table = turn_table(radix_size // 2, radix_size, radix_size)
    y_real = contract_front(cos_table, grid)
    y_imag = -contract_front(sin_table, grid)
    return twist_forward(y_real, y_imag, length, leading)


def untwist(z_real, z_imag, length):
    radix_size, inner_len = z_real.shape[-2:]
    cos_twist, sin_twist = turn_table(radix_size, inner_len, length)
    return (z_real * cos_twist - z_imag * sin_twist, z_imag * cos_twist + z_real * sin_twist)


def inverse(re_part, im_part):
    length = re_part.shape[-1]
    leading = re_part.shape[:-1]
    radix_size = split_of(length)
    if radix_size == 1:
        return base_transform(re_part, im_part, 1.0)
    inner_len = length // radix_size
    z_real, z_imag = inverse(
        re_part.reshape(leading + (radix_size, inner_len)),
        im_part.reshape(leading + (radix_size, inner_len)),
    )
    y_real, y_imag = untwist(z_real, z_imag, length)
    cos_table, sin_table = turn_table(radix_size, radix_size, radix_size)
    x_real = contract_front(cos_table, y_real) - contract_front(sin_table, y_imag)
    x_imag = contract_front(cos_table, y_imag) + contract_front(sin_table, y_real)
    return (x_real.reshape(leading + (length,)), x_imag.reshape(leading + (length,)))


def inverse_half(re_part, im_part):
    length = re_part.shape[-1]
    leading = re_part.shape[:-1]
    radix_size = split_of(length)
    inner_len = length // radix_size
    z_real, z_imag = inverse(
        re_part.reshape(leading + (radix_size, inner_len)),
        im_part.reshape(leading + (radix_size, inner_len)),
    )
    y_real, y_imag = untwist(z_real, z_imag, length)
    cos_table, sin_table = turn_table(radix_size, radix_size // 2, radix_size)
    x_real = contract_front(cos_table, y_real) - contract_front(sin_table, y_imag)
    x_imag = contract_front(cos_table, y_imag) + contract_front(sin_table, y_real)
    return (x_real.reshape(leading + (length // 2,)), x_imag.reshape(leading + (length // 2,)))


def body(query_stream, key_stream, value_stream, cotangent, filters):
    local_ch, length = query_stream.shape
    filter_count = filters.shape[0]
    ctx_count = lax.axis_size("ctx")
    per_device = local_ch // ctx_count
    seq_len = length * ctx_count
    padded_len = 2 * seq_len
    streams = jnp.stack([query_stream, key_stream, value_stream, cotangent], axis=0)
    arrived = lax.all_to_all(streams, "ctx", split_axis=1, concat_axis=2, tiled=True)
    queries = arrived[0].astype(jnp.float32)
    key_data = arrived[1].astype(jnp.float32)
    value_data = arrived[2].astype(jnp.float32)
    cot_data = arrived[3].astype(jnp.float32)
    repeated = jnp.tile(filters, (local_ch // filter_count, 1))
    filter_full = lax.all_to_all(repeated, "ctx", split_axis=0, concat_axis=1, tiled=True)
    product = key_data * value_data
    adjoint = cot_data * queries
    spec_real, spec_imag = forward_padded(jnp.concatenate([product, adjoint, filter_full], axis=0))
    prod_real, prod_imag = (spec_real[:per_device], spec_imag[:per_device])
    adj_real = spec_real[per_device : 2 * per_device]
    adj_imag = spec_imag[per_device : 2 * per_device]
    filt_real, filt_imag = (spec_real[2 * per_device :], spec_imag[2 * per_device :])
    mix_real = filt_real * prod_real - filt_imag * prod_imag
    mix_imag = filt_real * prod_imag + filt_imag * prod_real
    back_real = filt_real * adj_real + filt_imag * adj_imag
    back_imag = filt_real * adj_imag - filt_imag * adj_real
    corr_real = adj_real * prod_real + adj_imag * prod_imag
    corr_imag = adj_imag * prod_real - adj_real * prod_imag
    joint_real = jnp.concatenate([mix_real - back_imag, corr_real], axis=0)
    joint_imag = jnp.concatenate([mix_imag + back_real, corr_imag], axis=0)
    out_real, out_imag = inverse_half(joint_real, joint_imag)
    inv_scale = 1.0 / padded_len
    conv_out = out_real[:per_device] * inv_scale
    conv_back = out_imag[:per_device] * inv_scale
    filter_rows = out_real[per_device:] * inv_scale
    returned = lax.all_to_all(
        jnp.stack([conv_out, conv_back], axis=0), "ctx", split_axis=2, concat_axis=1, tiled=True
    )
    query_grad = (cotangent.astype(jnp.float32) * returned[0]).astype(jnp.bfloat16)
    key_grad = (returned[1] * value_stream.astype(jnp.float32)).astype(jnp.bfloat16)
    value_grad = (returned[1] * key_stream.astype(jnp.float32)).astype(jnp.bfloat16)
    grad_scale = 1.0 / math.sqrt(GROUP * seq_len)
    base_rows = lax.all_to_all(filter_rows, "ctx", split_axis=1, concat_axis=0, tiled=True)
    folded = base_rows.reshape(local_ch // filter_count, filter_count, length).sum(axis=0)
    filter_grad = lax.psum(folded, "chan") * grad_scale
    return (query_grad, key_grad, value_grad, filter_grad)


def solution(mesh):
    in_specs = (
        P("chan", ("groups", "ctx")),
        P("chan", ("groups", "ctx")),
        P("chan", ("groups", "ctx")),
        P("chan", ("groups", "ctx")),
        P(None, "ctx"),
    )
    out_specs = (
        P("chan", ("groups", "ctx")),
        P("chan", ("groups", "ctx")),
        P("chan", ("groups", "ctx")),
        P(None, ("groups", "ctx")),
    )
    chosen = body
    if mesh.shape["ctx"] == 4:
        chosen = blocked_body
    return jax.shard_map(chosen, mesh=mesh, in_specs=in_specs, out_specs=out_specs, check_vma=False)
```

```python
import functools
import math

import jax
import jax.numpy as jnp
import numpy as np
from jax import lax
from jax.experimental import pallas as pl
from jax.experimental.pallas import tpu as pltpu
from jax.sharding import PartitionSpec as P

GROUP = 16
MESH = pl.DeviceIdType.MESH
ROWS = 16


def half_tables(block):
    span = np.arange(block, dtype=np.int64)
    turned = ((2 * span[None, :] + 1) * span[:, None]) % (4 * block)
    angle = turned.astype(np.float64) * (math.pi / (2 * block))
    ahead = np.concatenate([np.cos(angle), -np.sin(angle)], axis=1).astype(np.float32)
    back = (np.concatenate([np.cos(angle).T, -np.sin(angle).T], axis=0) / block).astype(np.float32)

    def parts(table):
        high = table.astype(jnp.bfloat16)
        low = (table - high.astype(np.float32)).astype(jnp.bfloat16)
        return high, low

    ahead_high, ahead_low = parts(ahead)
    back_high, back_low = parts(back)
    return (
        np.concatenate([ahead_high, ahead_high, ahead_low], axis=0),
        np.concatenate([back_high, back_high, back_low], axis=0),
    )


def ctx_kernel(
    nchan,
    q_far,
    k_far,
    v_far,
    c_far,
    filt_far,
    ahead_far,
    back_far,
    qg_ref,
    kg_ref,
    vg_ref,
    fg_ref,
    q_ref,
    k_ref,
    v_ref,
    c_ref,
    filt_ref,
    ahead_ref,
    back_ref,
    fg_loc,
    fg_stage,
    fg_part,
    fg_ctx,
    fg_fin,
    pair_p,
    pair_a,
    landed,
    filt_all,
    gains,
    spec,
    prep,
    corr,
    agg_out,
    agg_in,
    send_sem,
    recv_sem,
    filt_send,
    filt_recv,
    spread_send,
    spread_recv,
    agg_send,
    agg_recv,
    near_sem,
    sum_send,
    sum_recv,
    own_send,
    own_recv,
    fin_send,
    fin_recv,
):
    copies, fcount, block = q_ref.shape
    chunks = nchan
    quarter = fcount // nchan
    crows = copies * quarter
    me = lax.axis_index("ctx")
    mine = lax.axis_index("chan")
    f32, bf16 = jnp.float32, jnp.bfloat16

    near = [
        pltpu.make_async_copy(src, dst, near_sem.at[at])
        for at, (src, dst) in enumerate(
            (
                (filt_far, filt_ref),
                (k_far, k_ref),
                (v_far, v_ref),
                (c_far, c_ref),
                (q_far, q_ref),
                (ahead_far, ahead_ref),
                (back_far, back_ref),
            )
        )
    ]
    for copy in near:
        copy.start()
    barrier = pltpu.get_barrier_semaphore()
    for step in range(1, 4):
        pl.semaphore_signal(
            barrier, inc=1, device_id={"ctx": lax.rem(me + step, 4)}, device_id_type=MESH
        )
    for step in range(1, nchan):
        pl.semaphore_signal(
            barrier, inc=1, device_id={"chan": lax.rem(mine + step, nchan)}, device_id_type=MESH
        )

    def first_row(chunk):
        return pl.multiple_of(lax.rem(mine + 1 + chunk, nchan) * quarter, quarter)

    def rows_of(chunk):
        return pl.ds(first_row(chunk), quarter)

    def split_into(dest, rows, left, right):
        val = left.astype(f32) * right.astype(f32)
        high = val.astype(bf16)
        dest[:, rows, 0:block] = high
        dest[:, rows, block : 2 * block] = (val - high.astype(f32)).astype(bf16)

    def make_pairs(dest, left, right, chunk):
        @pl.loop(0, quarter // ROWS)
        def _(i):
            rows = pl.ds(pl.multiple_of(first_row(chunk) + i * ROWS, ROWS), ROWS)
            split_into(dest, rows, left[:, rows, :], right[:, rows, :])

    for copy in near[:5]:
        copy.wait()
    pl.semaphore_wait(barrier, 3 + nchan - 1)

    def move(source, chunk, slot, target):
        rows = rows_of(chunk)
        return pltpu.make_async_remote_copy(
            src_ref=source.at[:, rows, :],
            dst_ref=landed.at[slot, :, rows, :],
            send_sem=send_sem.at[slot, chunk],
            recv_sem=recv_sem.at[slot, chunk],
            device_id={"ctx": target},
            device_id_type=MESH,
        )

    def filt_move(owner, target):
        rows = pl.ds(pl.multiple_of(mine * quarter, quarter), quarter)
        return pltpu.make_async_remote_copy(
            src_ref=filt_ref.at[rows, :],
            dst_ref=filt_all.at[owner, rows, :],
            send_sem=filt_send.at[target],
            recv_sem=filt_recv.at[owner],
            device_id={"ctx": target},
            device_id_type=MESH,
        )

    def spread(owner, step):
        rows = pl.ds(pl.multiple_of(mine * quarter, quarter), quarter)
        return pltpu.make_async_remote_copy(
            src_ref=filt_all.at[owner, rows, :],
            dst_ref=filt_all.at[owner, rows, :],
            send_sem=spread_send.at[owner, step],
            recv_sem=spread_recv.at[owner, step],
            device_id={"chan": lax.rem(mine + step, nchan)},
            device_id_type=MESH,
        )

    def agg_move(chunk, target):
        rows = rows_of(chunk)
        return pltpu.make_async_remote_copy(
            src_ref=agg_out.at[:, rows, :],
            dst_ref=agg_in.at[:, rows, :],
            send_sem=agg_send.at[chunk],
            recv_sem=agg_recv.at[chunk],
            device_id={"ctx": target},
            device_id_type=MESH,
        )

    def sum_move(blocks, step):
        peer = lax.rem(mine + step, nchan)
        return pltpu.make_async_remote_copy(
            src_ref=fg_loc.at[step, blocks, :, :],
            dst_ref=fg_stage.at[step, blocks, :, :],
            send_sem=sum_send.at[step],
            recv_sem=sum_recv.at[step],
            device_id={"chan": peer},
            device_id_type=MESH,
        )

    def own_move(target, source):
        return pltpu.make_async_remote_copy(
            src_ref=fg_part.at[target],
            dst_ref=fg_ctx.at[source],
            send_sem=own_send.at[target],
            recv_sem=own_recv.at[source],
            device_id={"ctx": target},
            device_id_type=MESH,
        )

    def fin_move(step):
        rows = pl.ds(pl.multiple_of(mine * quarter, quarter), quarter)
        return pltpu.make_async_remote_copy(
            src_ref=fg_fin.at[rows, :],
            dst_ref=fg_fin.at[rows, :],
            send_sem=fin_send.at[step],
            recv_sem=fin_recv.at[step],
            device_id={"chan": lax.rem(mine + step, nchan)},
            device_id_type=MESH,
        )

    def ahead(pairs):
        high = pairs[:, 0:block]
        return jnp.dot(pairs, ahead_ref[0 : 2 * block, :], preferred_element_type=f32) + jnp.dot(
            high, ahead_ref[2 * block : 3 * block, :], preferred_element_type=f32
        )

    def inverse_of(which):
        val = jnp.dot(
            prep[which, :, :], back_ref[0 : 4 * block, :], preferred_element_type=f32
        ) + jnp.dot(
            prep[which, :, 0 : 2 * block],
            back_ref[4 * block : 6 * block, :],
            preferred_element_type=f32,
        )
        return val.reshape(copies, quarter, block)

    def put_prep(which, rows, re, im):
        for place, val in ((0, re), (block, im)):
            high = val.astype(bf16)
            prep[which, rows, place : place + block] = high
            prep[which, rows, 2 * block + place : 3 * block + place] = (
                val - high.astype(f32)
            ).astype(bf16)

    def sign_of():
        col = lax.broadcasted_iota(jnp.int32, (ROWS, block), 1)
        return (1 - 2 * lax.rem(col, 2)).astype(f32)

    def role(j):
        inner = j in (1, 2)
        lower = j < 2
        own_u = pair_p if lower else pair_a
        sends = []
        targets = {0: (1, 2, 3), 1: (2,), 2: (1,), 3: (2, 1)}[j]
        needs = {0: (), 1: (0, 2, 3), 2: (0, 1, 3), 3: (0,)}[j]
        for target in targets:
            copy = filt_move(j, target)
            copy.start()
            sends.append(copy)
        from_p, from_a = (pair_p, k_ref, v_ref), (pair_a, c_ref, q_ref)
        first, second = (from_p, from_a) if lower else (from_a, from_p)
        for chunk in range(chunks):
            make_pairs(*first, chunk)
            if inner:
                moves = [move(own_u, chunk, 1, 3 - j)]
            else:
                moves = [
                    move(own_u, chunk, 2, 2 if lower else 1),
                    move(own_u, chunk, 0, 1 if lower else 2),
                ]
            for copy in moves:
                copy.start()
                sends.append(copy)
        for chunk in range(chunks):
            make_pairs(*second, chunk)
        for copy in near[5:]:
            copy.wait()
        for owner in needs:
            filt_move(owner, j).wait_recv()
            for step in range(1, nchan):
                copy = spread(owner, step)
                copy.start()
                sends.append(copy)
        filt_all[j, :, :] = filt_ref[...]
        for owner in needs:
            for step in range(1, nchan):
                spread(owner, step).wait_recv()
        used = range(4) if inner else (0,)
        for owner in used:
            val = filt_all[owner, :, :]
            high = val.astype(bf16)
            low = (val - high.astype(f32)).astype(bf16)
            spec[owner, :, :] = ahead(jnp.concatenate([high, low], axis=1))

        @pl.loop(0, fcount // ROWS)
        def _(i):
            rows = pl.ds(pl.multiple_of(i * ROWS, ROWS), ROWS)
            sign = sign_of()
            for d in used:
                re, im = spec[d, rows, 0:block], spec[d, rows, block : 2 * block]
                if d:
                    re = re - sign * spec[d - 1, rows, block : 2 * block]
                    im = im + sign * spec[d - 1, rows, 0:block]
                gains[d, rows, 0:block] = re
                gains[d, rows, block : 2 * block] = im

        if inner:
            held_p = {1: (0, 1), 2: (0, 1, 2)}[j]
            held_a = {1: (1, 2, 3), 2: (2, 3)}[j]
        else:
            held_p, held_a = (j,), (j,)
        places = {}
        for i in held_p:
            places["p", i] = len(places)
        for i in held_a:
            places["a", i] = len(places)
        slots = {1: {("p", 0): 0, ("a", 2): 1, ("a", 3): 2}, 2: {("a", 3): 0, ("p", 1): 1, ("p", 0): 2}}
        slots = slots.get(j, {})
        pairs_fg = {
            0: ((0, 0),),
            1: ((1, 1), (0, 1), (1, 2), (1, 3)),
            2: ((2, 2), (2, 3), (0, 2), (0, 3)),
            3: ((3, 3),),
        }[j]

        scale = 1.0 / math.sqrt(GROUP * block * 4)
        blocks = pl.ds(0, len(used))
        for chunk in range(chunks):
            crow = rows_of(chunk)
            corr[...] = jnp.zeros(corr.shape, f32)
            for name, place in places.items():
                if name in slots:
                    move(own_u, chunk, slots[name], j).wait_recv()
                    spec[place, :, :] = ahead(landed[slots[name], :, crow, :].reshape(crows, 2 * block))
                else:
                    spec[place, :, :] = ahead(
                        (pair_p if name[0] == "p" else pair_a)[:, crow, :].reshape(crows, 2 * block)
                    )

            @pl.loop(0, crows // ROWS)
            def _(i):
                rows = pl.ds(pl.multiple_of(i * ROWS, ROWS), ROWS)
                place_in = lax.rem(i, quarter // ROWS) * ROWS
                frows = pl.ds(pl.multiple_of(first_row(chunk) + place_in, ROWS), ROWS)
                drows = pl.ds(pl.multiple_of(place_in, ROWS), ROWS)

                def load(name):
                    at = places[name]
                    return spec[at, rows, 0:block], spec[at, rows, block : 2 * block]

                def gain(d):
                    return gains[d, frows, 0:block], gains[d, frows, block : 2 * block]

                def mixed_to(target):
                    re = im = None
                    for src in held_p:
                        if src > target:
                            continue
                        pr, pi = load(("p", src))
                        gr, gi = gain(target - src)
                        r, m = pr * gr - pi * gi, pr * gi + pi * gr
                        re, im = (r, m) if re is None else (re + r, im + m)
                    return re, im

                def back_to(target):
                    re = im = None
                    for src in held_a:
                        if src < target:
                            continue
                        ar, ai = load(("a", src))
                        gr, gi = gain(src - target)
                        r, m = ar * gr + ai * gi, ai * gr - ar * gi
                        re, im = (r, m) if re is None else (re + r, im + m)
                    return re, im

                put_prep(0, rows, *mixed_to(j))
                put_prep(1, rows, *back_to(j))
                if j == 1:
                    put_prep(2, rows, *back_to(0))
                if j == 2:
                    put_prep(2, rows, *mixed_to(3))
                for src, dst in pairs_fg:
                    pr, pi = load(("p", src))
                    ar, ai = load(("a", dst))
                    d = dst - src
                    corr[d, drows, 0:block] += ar * pr + ai * pi
                    corr[d, drows, block : 2 * block] += ai * pr - ar * pi

            if inner:
                agg_out[:, crow, :] = inverse_of(2)
                copy = agg_move(chunk, 0 if lower else 3)
                copy.start()
                sends.append(copy)
            if j == 3:
                agg_out[:, crow, :] = inverse_of(0)
            else:
                qg_ref[:, crow, :] = (c_ref[:, crow, :].astype(f32) * inverse_of(0)).astype(bf16)
            if j == 0:
                agg_out[:, crow, :] = inverse_of(1)
            else:
                back = inverse_of(1)
                kg_ref[:, crow, :] = (back * v_ref[:, crow, :].astype(f32)).astype(bf16)
                vg_ref[:, crow, :] = (back * k_ref[:, crow, :].astype(f32)).astype(bf16)

            for b in used:

                @pl.loop(0, quarter // ROWS)
                def _(i):
                    rows = pl.ds(pl.multiple_of(i * ROWS, ROWS), ROWS)
                    re, im = corr[b, rows, 0:block], corr[b, rows, block : 2 * block]
                    if b + 1 in used:
                        sign = sign_of()
                        re = re + sign * corr[b + 1, rows, block : 2 * block]
                        im = im - sign * corr[b + 1, rows, 0:block]
                    put_prep(0, pl.ds(pl.multiple_of(b * quarter + i * ROWS, ROWS), ROWS), re, im)

            place = chunk + 1 if chunk < chunks - 1 else 0
            terms = inverse_of(0).reshape(crows, block) * scale
            for b in used:
                fg_loc[place, b, :, :] = terms[b * quarter : (b + 1) * quarter, :]
            if place:
                copy = sum_move(blocks, place)
                copy.start()
                sends.append(copy)

        my_rows = pl.ds(pl.multiple_of(mine * quarter, quarter), quarter)
        for step in range(1, nchan):
            sum_move(blocks, step).wait_recv()
        for b in used:
            total = fg_loc[0, b, :, :]
            for step in range(1, nchan):
                total = total + fg_stage[step, b, :, :]
            fg_part[b, :, :] = total
        for b in used:
            if b != j:
                copy = own_move(b, j)
                copy.start()
                sends.append(copy)

        if not inner:
            for chunk in range(chunks):
                crow = rows_of(chunk)
                agg_move(chunk, j).wait_recv()
                total = agg_out[:, crow, :] + agg_in[:, crow, :]
                if j == 3:
                    qg_ref[:, crow, :] = (c_ref[:, crow, :].astype(f32) * total).astype(bf16)
                else:
                    kg_ref[:, crow, :] = (total * v_ref[:, crow, :].astype(f32)).astype(bf16)
                    vg_ref[:, crow, :] = (total * k_ref[:, crow, :].astype(f32)).astype(bf16)
        total = fg_part[j, :, :] if j in used else None
        for src in {0: (1, 2, 3), 1: (2,), 2: (1,), 3: (1, 2)}[j]:
            own_move(j, src).wait_recv()
            term = fg_ctx[src, :, :]
            total = term if total is None else total + term
        fg_fin[my_rows, :] = total
        for step in range(1, nchan):
            copy = fin_move(step)
            copy.start()
            sends.append(copy)
        for step in range(1, nchan):
            fin_move(step).wait_recv()
        fg_ref[...] = fg_fin[...]
        for copy in sends:
            copy.wait_send()

    for j in range(4):
        pl.when(me == j)(functools.partial(role, j))


def blocked_body(query_stream, key_stream, value_stream, cotangent, filters):
    local_ch, block = query_stream.shape
    fcount = filters.shape[0]
    nchan = lax.axis_size("chan")
    copies = local_ch // fcount
    shape = (copies, fcount, block)
    ahead, back = half_tables(block)
    ahead = jnp.asarray(ahead)
    back = jnp.asarray(back)
    vmem = pl.BlockSpec(memory_space=pltpu.VMEM)
    stream = jax.ShapeDtypeStruct(shape, jnp.bfloat16)
    dma = pltpu.SemaphoreType.DMA
    quarter = fcount // nchan
    chunks, crows = nchan, copies * quarter
    *grads, filter_grad = pl.pallas_call(
        functools.partial(ctx_kernel, nchan),
        out_shape=(
            stream,
            stream,
            stream,
            jax.ShapeDtypeStruct((fcount, block), jnp.float32),
        ),
        in_specs=[pl.BlockSpec(memory_space=pltpu.HBM)] * 7,
        out_specs=(vmem,) * 4,
        scratch_shapes=[
            pltpu.VMEM(shape, jnp.bfloat16),
            pltpu.VMEM(shape, jnp.bfloat16),
            pltpu.VMEM(shape, jnp.bfloat16),
            pltpu.VMEM(shape, jnp.bfloat16),
            pltpu.VMEM((fcount, block), jnp.float32),
            pltpu.VMEM((3 * block, 2 * block), jnp.bfloat16),
            pltpu.VMEM((6 * block, block), jnp.bfloat16),
            pltpu.VMEM((nchan, 4, quarter, block), jnp.float32),
            pltpu.VMEM((nchan, 4, quarter, block), jnp.float32),
            pltpu.VMEM((4, quarter, block), jnp.float32),
            pltpu.VMEM((4, quarter, block), jnp.float32),
            pltpu.VMEM((fcount, block), jnp.float32),
            pltpu.VMEM((copies, fcount, 2 * block), jnp.bfloat16),
            pltpu.VMEM((copies, fcount, 2 * block), jnp.bfloat16),
            pltpu.VMEM((3, copies, fcount, 2 * block), jnp.bfloat16),
            pltpu.VMEM((4, fcount, block), jnp.float32),
            pltpu.VMEM((4, fcount, 2 * block), jnp.float32),
            pltpu.VMEM((5, max(crows, fcount), 2 * block), jnp.float32),
            pltpu.VMEM((3, crows, 4 * block), jnp.bfloat16),
            pltpu.VMEM((4, quarter, 2 * block), jnp.float32),
            pltpu.VMEM(shape, jnp.float32),
            pltpu.VMEM(shape, jnp.float32),
            dma((3, chunks)),
            dma((3, chunks)),
            dma((4,)),
            dma((4,)),
            dma((4, nchan)),
            dma((4, nchan)),
            dma((chunks,)),
            dma((chunks,)),
            dma((7,)),
            dma((nchan,)),
            dma((nchan,)),
            dma((4,)),
            dma((4,)),
            dma((nchan,)),
            dma((nchan,)),
        ],
        compiler_params=pltpu.CompilerParams(
            collective_id=0, has_side_effects=True, vmem_limit_bytes=60 * 1024 * 1024
        ),
        cost_estimate=pl.CostEstimate(flops=8 * 10**9, bytes_accessed=8 * 10**6, transcendentals=0),
    )(
        *(x.reshape(shape) for x in (query_stream, key_stream, value_stream, cotangent)),
        filters,
        ahead,
        back,
    )
    return (*(x.reshape(local_ch, block) for x in grads), filter_grad)


highest_mode = lax.Precision.HIGHEST


def turn_table(row_count, col_count, modulus):
    row_span = jnp.arange(row_count, dtype=jnp.int32)
    col_span = jnp.arange(col_count, dtype=jnp.int32)
    turned = row_span[:, None] * col_span[None, :] % modulus
    angle_vals = turned.astype(jnp.float32) * (2.0 * math.pi / modulus)
    return (jnp.cos(angle_vals), jnp.sin(angle_vals))


def split_of(length):
    for candidate in range(32, 1, -1):
        if (
            length % candidate == 0
            and length // candidate >= 128
            and (length // candidate % 128 == 0)
        ):
            return candidate
    return 1


def contract_front(table, operand):
    return jnp.einsum("ac,...ab->...cb", table, operand, precision=highest_mode)


def base_transform(re_part, im_part, sign_value):
    length = re_part.shape[-1]
    cos_table, sin_table = turn_table(length, length, length)
    turn_imag = sign_value * sin_table
    summed = jnp.einsum("...t,tk->...k", re_part + im_part, cos_table, precision=highest_mode)
    left_term = jnp.einsum("...t,tk->...k", re_part, turn_imag - cos_table, precision=highest_mode)
    second = jnp.einsum("...t,tk->...k", im_part, cos_table + turn_imag, precision=highest_mode)
    return (summed - second, summed + left_term)


def twist_forward(y_real, y_imag, length, leading):
    radix_size, inner_len = y_real.shape[-2:]
    cos_twist, sin_twist = turn_table(radix_size, inner_len, length)
    tw_real = y_real * cos_twist + y_imag * sin_twist
    tw_imag = y_imag * cos_twist - y_real * sin_twist
    z_real, z_imag = forward(tw_real, tw_imag)
    return (z_real.reshape(leading + (length,)), z_imag.reshape(leading + (length,)))


def forward(re_part, im_part):
    length = re_part.shape[-1]
    leading = re_part.shape[:-1]
    radix_size = split_of(length)
    if radix_size == 1:
        return base_transform(re_part, im_part, -1.0)
    inner_len = length // radix_size
    re_grid = re_part.reshape(leading + (radix_size, inner_len))
    im_grid = im_part.reshape(leading + (radix_size, inner_len))
    cos_table, sin_table = turn_table(radix_size, radix_size, radix_size)
    y_real = contract_front(cos_table, re_grid) + contract_front(sin_table, im_grid)
    y_imag = contract_front(cos_table, im_grid) - contract_front(sin_table, re_grid)
    return twist_forward(y_real, y_imag, length, leading)


def forward_padded(signal):
    half_len = signal.shape[-1]
    length = 2 * half_len
    leading = signal.shape[:-1]
    radix_size = split_of(length)
    inner_len = length // radix_size
    grid = signal.reshape(leading + (radix_size // 2, inner_len))
    cos_table, sin_table = turn_table(radix_size // 2, radix_size, radix_size)
    y_real = contract_front(cos_table, grid)
    y_imag = -contract_front(sin_table, grid)
    return twist_forward(y_real, y_imag, length, leading)


def untwist(z_real, z_imag, length):
    radix_size, inner_len = z_real.shape[-2:]
    cos_twist, sin_twist = turn_table(radix_size, inner_len, length)
    return (z_real * cos_twist - z_imag * sin_twist, z_imag * cos_twist + z_real * sin_twist)


def inverse(re_part, im_part):
    length = re_part.shape[-1]
    leading = re_part.shape[:-1]
    radix_size = split_of(length)
    if radix_size == 1:
        return base_transform(re_part, im_part, 1.0)
    inner_len = length // radix_size
    z_real, z_imag = inverse(
        re_part.reshape(leading + (radix_size, inner_len)),
        im_part.reshape(leading + (radix_size, inner_len)),
    )
    y_real, y_imag = untwist(z_real, z_imag, length)
    cos_table, sin_table = turn_table(radix_size, radix_size, radix_size)
    x_real = contract_front(cos_table, y_real) - contract_front(sin_table, y_imag)
    x_imag = contract_front(cos_table, y_imag) + contract_front(sin_table, y_real)
    return (x_real.reshape(leading + (length,)), x_imag.reshape(leading + (length,)))


def inverse_half(re_part, im_part):
    length = re_part.shape[-1]
    leading = re_part.shape[:-1]
    radix_size = split_of(length)
    inner_len = length // radix_size
    z_real, z_imag = inverse(
        re_part.reshape(leading + (radix_size, inner_len)),
        im_part.reshape(leading + (radix_size, inner_len)),
    )
    y_real, y_imag = untwist(z_real, z_imag, length)
    cos_table, sin_table = turn_table(radix_size, radix_size // 2, radix_size)
    x_real = contract_front(cos_table, y_real) - contract_front(sin_table, y_imag)
    x_imag = contract_front(cos_table, y_imag) + contract_front(sin_table, y_real)
    return (x_real.reshape(leading + (length // 2,)), x_imag.reshape(leading + (length // 2,)))


def body(query_stream, key_stream, value_stream, cotangent, filters):
    local_ch, length = query_stream.shape
    filter_count = filters.shape[0]
    ctx_count = lax.axis_size("ctx")
    per_device = local_ch // ctx_count
    seq_len = length * ctx_count
    padded_len = 2 * seq_len
    streams = jnp.stack([query_stream, key_stream, value_stream, cotangent], axis=0)
    arrived = lax.all_to_all(streams, "ctx", split_axis=1, concat_axis=2, tiled=True)
    queries = arrived[0].astype(jnp.float32)
    key_data = arrived[1].astype(jnp.float32)
    value_data = arrived[2].astype(jnp.float32)
    cot_data = arrived[3].astype(jnp.float32)
    repeated = jnp.tile(filters, (local_ch // filter_count, 1))
    filter_full = lax.all_to_all(repeated, "ctx", split_axis=0, concat_axis=1, tiled=True)
    product = key_data * value_data
    adjoint = cot_data * queries
    spec_real, spec_imag = forward_padded(jnp.concatenate([product, adjoint, filter_full], axis=0))
    prod_real, prod_imag = (spec_real[:per_device], spec_imag[:per_device])
    adj_real = spec_real[per_device : 2 * per_device]
    adj_imag = spec_imag[per_device : 2 * per_device]
    filt_real, filt_imag = (spec_real[2 * per_device :], spec_imag[2 * per_device :])
    mix_real = filt_real * prod_real - filt_imag * prod_imag
    mix_imag = filt_real * prod_imag + filt_imag * prod_real
    back_real = filt_real * adj_real + filt_imag * adj_imag
    back_imag = filt_real * adj_imag - filt_imag * adj_real
    corr_real = adj_real * prod_real + adj_imag * prod_imag
    corr_imag = adj_imag * prod_real - adj_real * prod_imag
    joint_real = jnp.concatenate([mix_real - back_imag, corr_real], axis=0)
    joint_imag = jnp.concatenate([mix_imag + back_real, corr_imag], axis=0)
    out_real, out_imag = inverse_half(joint_real, joint_imag)
    inv_scale = 1.0 / padded_len
    conv_out = out_real[:per_device] * inv_scale
    conv_back = out_imag[:per_device] * inv_scale
    filter_rows = out_real[per_device:] * inv_scale
    returned = lax.all_to_all(
        jnp.stack([conv_out, conv_back], axis=0), "ctx", split_axis=2, concat_axis=1, tiled=True
    )
    query_grad = (cotangent.astype(jnp.float32) * returned[0]).astype(jnp.bfloat16)
    key_grad = (returned[1] * value_stream.astype(jnp.float32)).astype(jnp.bfloat16)
    value_grad = (returned[1] * key_stream.astype(jnp.float32)).astype(jnp.bfloat16)
    grad_scale = 1.0 / math.sqrt(GROUP * seq_len)
    base_rows = lax.all_to_all(filter_rows, "ctx", split_axis=1, concat_axis=0, tiled=True)
    folded = base_rows.reshape(local_ch // filter_count, filter_count, length).sum(axis=0)
    filter_grad = lax.psum(folded, "chan") * grad_scale
    return (query_grad, key_grad, value_grad, filter_grad)


def solution(mesh):
    in_specs = (
        P("chan", ("groups", "ctx")),
        P("chan", ("groups", "ctx")),
        P("chan", ("groups", "ctx")),
        P("chan", ("groups", "ctx")),
        P(None, "ctx"),
    )
    out_specs = (
        P("chan", ("groups", "ctx")),
        P("chan", ("groups", "ctx")),
        P("chan", ("groups", "ctx")),
        P(None, ("groups", "ctx")),
    )
    chosen = body
    if mesh.shape["ctx"] == 4:
        chosen = blocked_body
    return jax.shard_map(chosen, mesh=mesh, in_specs=in_specs, out_specs=out_specs, check_vma=False)
```
